32 devices in a mesh: groups: 2 (over x), layer: 4 (over z), iface: 4 (over y, core).
Axes of the slice: x: 2, y: 2, z: 4, core: 2. Of those that a mesh axis runs over, the one named last changes fastest.
Arguments:
- top_trace: bfloat16 [6, 2, 8192, 128], P('groups', None, 'iface'), parts along dimension 0, may hold values from -6 to 6
- sources: bfloat16 [4, 8, 2, 8192, 128], P('layer', 'groups', None, 'iface'), parts along dimension 1, may hold values from -6 to 6
- near_blocks: bfloat16 [4, 2, 32, 8, 256, 256], P('layer', None, 'iface'), may hold values from -0.0625 to 0.0625
- near_index: int32 [32, 8], P('iface'), may hold values from 0 to 31, as said below
- far_left: bfloat16 [4, 2, 64, 8192], P('layer', None, None, 'iface'), may hold values from -0.25 to 0.25
- far_right: bfloat16 [4, 2, 64, 8192], P('layer', None, None, 'iface'), may hold values from -0.046875 to 0.046875
- assign: int32 [4, 3], replicated, may hold values from 0 to 3
Outputs:
- traces: bfloat16 [4, 6, 2, 8192, 128], P('layer', 'groups', None, 'iface'), parts along dimension 1
The draws below stay inside these ranges and needn't reach their ends.
There are 2 independent parts, one for each index of `groups`. The reference program is written for one: setup_inputs(seed, part) draws one part's arguments, and reference() takes and returns one part's arrays. A program takes and returns all parts, laid end to end along the dimension named above; an argument that names none is the same for every part. Nothing has to cross between parts.
Inputs may be any that keep to these rules, and one draw needn't show every extreme that they name: near_index[b, k] = clip(b + o, 0, 8192 / 256 - 1) with the offsets o of a row distinct in -4 .. 4.
All inputs are finite; a program needn't handle non-finite values.
Results may differ from the reference program's by a relative error of at most 0.012.
Values may be sent and summed in bfloat16 or wider, within the bound.
No kernel may reach another device: no remote copies, remote signals or barrier semaphores. Data moves between devices by JAX's collectives and lax.ppermute only.
A program may use at most 128 MiB of HBM per device.

```python
import jax
import jax.numpy as jnp

NI = 8192
BLK = 256
NEAR = 8
BAND = 4
RANK = 64
P_SIZE = 128
PANELS = 3
BANK = 4
LAYERS = 4


def draw_near_index(key, part):
    count = NI // BLK
    width = 2 * BAND + 1
    scores = jax.random.randint(key, (count, width), 0, 1 << 20) * width + jnp.arange(width)[None, :]
    order = jnp.argsort(scores, axis=1, stable=True)
    offsets = order[:, :NEAR] - BAND
    return jnp.clip(jnp.arange(count)[:, None] + offsets, 0, count - 1).astype(jnp.int32)


def touch_ends(array, own_key, low, high):
    place = [jax.random.randint(jax.random.fold_in(own_key, axis), (), 0, length) for axis, length in enumerate(array.shape)]
    main_axis = array.shape.index(max(array.shape))
    neighbour = place[:main_axis] + [(place[main_axis] + 1) % array.shape[main_axis]] + place[main_axis + 1:]
    return array.at[tuple(place)].set(low).at[tuple(neighbour)].set(high)


def block_scale(key, extent, pieces, least, largest):
    gain = 1.0
    for position, parts in pieces:
        draws = jax.random.uniform(jax.random.fold_in(jax.random.fold_in(key, 6), position), (parts,), jnp.float32, least / len(pieces), largest / len(pieces))
        gain = gain * jnp.repeat(jnp.exp(draws), extent[position] // parts).reshape((-1,) + (1,) * (len(extent) - 1 - position))
    return gain


def normal_values(rng, shape, deviation, bound, pieces=(), held_as=jnp.bfloat16):
    drawn = deviation * jax.random.normal(rng, shape, jnp.float32)
    if pieces:
        drawn = drawn * block_scale(rng, shape, pieces, -0.22, 0.18)
    return jnp.clip(drawn, -bound, bound).astype(held_as)


def setup_inputs(seed: int = 0, part: int = 0) -> dict:
    seeds = jax.random.split(jax.random.key(seed), 8)
    own_keys = jax.random.split(jax.random.fold_in(seeds[7], part), 8)
    return {
        "top_trace": normal_values(own_keys[0], (PANELS, 2, NI, P_SIZE), 1.0, 6.0, ((2, 4),)),
        "sources": normal_values(own_keys[1], (LAYERS, BANK, 2, NI, P_SIZE), 1.0, 6.0, ((0, 4), (3, 4))),
        "near_blocks": normal_values(seeds[2], (LAYERS, 2, NI // BLK, NEAR, BLK, BLK), (4 * NEAR * BLK) ** -0.5, 0.0625, ((0, 4), (2, 4))),
        "near_index": draw_near_index(jax.random.fold_in(seeds[7], 71), part),
        "far_left": normal_values(seeds[4], (LAYERS, 2, RANK, NI), (8 * RANK) ** -0.5, 0.25, ((0, 4), (3, 4))),
        "far_right": normal_values(seeds[5], (LAYERS, 2, RANK, NI), (2 * NI) ** -0.5, 0.046875, ((0, 4), (3, 4))),
        "assign": touch_ends(jax.random.randint(seeds[6], (LAYERS, PANELS), 0, BANK), jax.random.fold_in(seeds[6], 1), 0, BANK - 1).astype(jnp.int32),
    }


def near_apply(trace_in, blocks_mat, near_index):
    count = NI // BLK
    shaped = trace_in.reshape(2, count, BLK, P_SIZE).astype(jnp.float32)
    picked = shaped[:, near_index]
    mats = blocks_mat.astype(jnp.float32)
    part_real = jnp.einsum("jkab,cjkbp->cjap", mats[0], picked)
    part_imag = jnp.einsum("jkab,cjkbp->cjap", mats[1], picked)
    result = jnp.stack([part_real[0] - part_imag[1], part_real[1] + part_imag[0]])
    return result.reshape(2, NI, P_SIZE)


def far_apply(trace_in, left_mat, right_mat):
    def mult(mat, vec):
        return jnp.dot(mat, vec, preferred_element_type=jnp.float32)

    partial_value = jnp.stack([mult(right_mat[0], trace_in[0]) - mult(right_mat[1], trace_in[1]),
                         mult(right_mat[0], trace_in[1]) + mult(right_mat[1], trace_in[0])])
    coefficient = partial_value.astype(jnp.bfloat16)

    def lift(mat, vec):
        return jnp.einsum("ri,rp->ip", mat.astype(jnp.float32), vec.astype(jnp.float32))

    return jnp.stack([lift(left_mat[0], coefficient[0]) - lift(left_mat[1], coefficient[1]),
                      lift(left_mat[0], coefficient[1]) + lift(left_mat[1], coefficient[0])])


def reference(top_trace, sources, near_blocks, near_index, far_left, far_right, assign):
    per_layer = []
    for layer_pos in range(LAYERS):
        per_layer.append([])
    for panel_idx in range(PANELS):
        current = top_trace[panel_idx]
        for layer_pos in range(LAYERS):
            near_term = near_apply(current, near_blocks[layer_pos], near_index)
            far_term = far_apply(current, far_left[layer_pos], far_right[layer_pos])
            source_term = sources[layer_pos, assign[layer_pos, panel_idx]].astype(jnp.float32)
            current = (near_term + far_term + source_term).astype(jnp.bfloat16)
            per_layer[layer_pos].append(current)
    return jnp.stack([jnp.stack(items) for items in per_layer])
```

```python
import functools

import jax
import jax.numpy as jnp
from jax import lax
from jax.experimental import pallas as pl
from jax.experimental.pallas import tpu as pltpu
from jax.sharding import PartitionSpec as P

BLK = 256
BAND = 4
PARTS = 2
VMEM_LIMIT = 24 * 1024 * 1024


def turned(packed):
    half = packed.shape[1] // 2
    return jnp.concatenate([-packed[:, half:], packed[:, :half]], axis=1)


def near_terms(row, first, last, slot_ref, order_ref, blocks_ref, window_ref, turned_ref):
    total = None
    for k in range(first, last):
        start = pl.multiple_of(slot_ref[row, k] * BLK, BLK)
        k_pos = order_ref[row, k]
        part = jnp.dot(
            blocks_ref[0, row, k_pos], window_ref[pl.ds(start, BLK), :], preferred_element_type=jnp.float32
        )
        part += jnp.dot(
            blocks_ref[1, row, k_pos], turned_ref[pl.ds(start, BLK), :], preferred_element_type=jnp.float32
        )
        total = part if total is None else total + part
    return total


def own_kernel(
    with_store, early, part, scal_ref, slot_ref, order_ref, blocks_ref, entering_ref, bank_ref, *rest
):
    if with_store:
        first_ref, second_ref, _, acc_ref, out_ref, turned_ref, source_ref, panel_ref, sem = rest
    else:
        acc_ref, turned_ref, source_ref, sem = rest
    rows = acc_ref.shape[0]
    half = acc_ref.shape[1] // 2
    fetch = pltpu.make_async_copy(bank_ref.at[scal_ref[0]], source_ref, sem.at[0])
    fetch.start()
    if with_store:
        store = pltpu.make_async_copy(panel_ref, out_ref.at[0, scal_ref[1]], sem.at[1])

        @pl.when(scal_ref[2] == 1)
        def _():
            for comp in range(2):
                lanes = slice(comp * half, (comp + 1) * half)
                panel_ref[comp] = jnp.concatenate([first_ref[:rows, lanes], second_ref[:rows, lanes]], axis=1)
            store.start()

    turned_ref[...] = turned(entering_ref[:rows, :])
    lanes = slice(part * half, (part + 1) * half)
    for row in range(rows // BLK):
        at = slice(row * BLK, (row + 1) * BLK)
        value = near_terms(row, 0, early, slot_ref, order_ref, blocks_ref, entering_ref, turned_ref)
        if row == 0:
            fetch.wait()
        packed = jnp.concatenate([source_ref[0, at, lanes], source_ref[1, at, lanes]], axis=1).astype(jnp.float32)
        acc_ref[at, :] = packed if value is None else value + packed
    if with_store:

        @pl.when(scal_ref[2] == 1)
        def _():
            store.wait()


def rest_kernel(
    early, near, halo_rows, rank, slot_ref, order_ref, blocks_ref, acc_ref, entering_ref, left_ref, right_ref, *rest
):
    halo_refs = rest[: len(halo_rows)]
    sum_refs = rest[len(halo_rows) : -3]
    leaving_ref, window_ref, turned_ref = rest[-3:]
    rows, lanes = acc_ref.shape
    place = 0
    for ref, count in zip((entering_ref,) + halo_refs, (rows,) + halo_rows):
        value = ref[:count, :]
        window_ref[place : place + count, :] = value
        turned_ref[place : place + count, :] = turned(value)
        place += count
    coefficient = jnp.zeros((rank, lanes), jnp.float32)
    for ref, start in [(entering_ref, rows)] + list(zip(halo_refs, halo_rows)) + [(ref, 0) for ref in sum_refs]:
        for at in range(start, ref.shape[0], rank):
            coefficient += ref[at : at + rank, :].astype(jnp.float32)
    spread = jnp.concatenate([coefficient, turned(coefficient)], axis=0).astype(jnp.bfloat16)
    next_part = jnp.zeros((2 * rank, lanes), jnp.float32)
    for row in range(rows // BLK):
        at = slice(row * BLK, (row + 1) * BLK)
        value = near_terms(row, early, near, slot_ref, order_ref, blocks_ref, window_ref, turned_ref)
        value += jnp.dot(left_ref[at, :], spread, preferred_element_type=jnp.float32)
        value = (value + acc_ref[at, :]).astype(jnp.bfloat16)
        leaving_ref[at, :] = value
        next_part += jnp.dot(right_ref[:, at], value, preferred_element_type=jnp.float32)
    partial_value = next_part[:rank] + turned(next_part[rank:])
    upper = partial_value.astype(jnp.bfloat16)
    leaving_ref[rows : rows + rank, :] = upper
    leaving_ref[rows + rank :, :] = (partial_value - upper.astype(jnp.float32)).astype(jnp.bfloat16)


def store_kernel(scal_ref, first_ref, second_ref, _, out_ref, panel_ref, sem):
    rows, half = out_ref.shape[3], out_ref.shape[4] // 2

    @pl.when(scal_ref[2] == 1)
    def _():
        for comp in range(2):
            lanes = slice(comp * half, (comp + 1) * half)
            panel_ref[comp] = jnp.concatenate([first_ref[:rows, lanes], second_ref[:rows, lanes]], axis=1)
        store = pltpu.make_async_copy(panel_ref, out_ref.at[0, scal_ref[1]], sem.at[0])
        store.start()
        store.wait()


def shifted(block, axis, distance):
    devices = range(lax.axis_size(axis))
    route = [(i - distance, i) for i in devices if i - distance in devices]
    return lax.ppermute(block, axis, route)


def per_device(top_trace, sources, near_blocks, near_index, far_left, far_right, assign):
    panel_count, _, rows, columns = top_trace.shape
    rank = far_left.shape[2]
    near = near_index.shape[1]
    blocks_dev = rows // BLK
    width = columns // PARTS
    lanes = 2 * width
    reach_rows = BAND * BLK
    reach_shards = -(-reach_rows // rows)
    layer_count = lax.axis_size("layer")
    layer_pos = lax.axis_index("layer")
    iface_count = lax.axis_size("iface")
    iface_pos = lax.axis_index("iface")
    chunk_count = panel_count * PARTS
    tick_count = chunk_count + 2 * (layer_count - 1)
    in_pairs = iface_count == 4 and reach_rows <= rows
    is_odd = iface_pos % 2

    offset = near_index - iface_pos * blocks_dev
    own = jnp.logical_and(offset >= 0, offset < blocks_dev)
    if in_pairs:
        below = jnp.where(is_odd == 1, blocks_dev, blocks_dev + BAND)
        above = jnp.where(is_odd == 1, blocks_dev + BAND, blocks_dev)
        slot = jnp.where(own, offset, jnp.where(offset < 0, below + offset + BAND, above + offset - blocks_dev))
    else:
        shard = jnp.floor_divide(offset, blocks_dev)
        group = jnp.where(shard < 0, -shard, jnp.where(shard > 0, reach_shards + shard, 0))
        slot = group * blocks_dev + offset - shard * blocks_dev
    key = jnp.where(own, 0, near) + jnp.arange(near)[None, :]
    place = jnp.sum(key[:, None, :] < key[:, :, None], axis=2)
    hit = place[:, None, :] == jnp.arange(near)[None, :, None]
    slot = jnp.sum(jnp.where(hit, slot[:, None, :], 0), axis=2).astype(jnp.int32)
    order = jnp.sum(jnp.where(hit, jnp.arange(near)[None, None, :], 0), axis=2).astype(jnp.int32)
    own_least = min(min(b, BAND) + min(blocks_dev - 1 - b, BAND) + 1 for b in range(blocks_dev))
    early = max(0, min(near, own_least - (2 * BAND + 1 - near)))

    blocks_mat = near_blocks[0]
    left_mat = far_left[0].reshape(2 * rank, rows).T
    next_right = shifted(far_right, "layer", -1)[0].reshape(2 * rank, rows)
    bank = sources[0]

    top = top_trace.reshape(panel_count, 2, rows, PARTS, width).transpose(0, 3, 2, 1, 4)
    top = top.reshape(chunk_count, rows, lanes)
    both = jnp.einsum(
        "ri,qip->qrp", far_right[0].reshape(2 * rank, rows), top, preferred_element_type=jnp.float32
    )
    low = both[:, rank:]
    first_part = both[:, :rank] + jnp.concatenate([-low[:, :, width:], low[:, :, :width]], axis=2)
    upper = lax.reduce_precision(first_part, 8, 7)
    top = jnp.concatenate(
        [top, upper.astype(jnp.bfloat16), (first_part - upper).astype(jnp.bfloat16)], axis=1
    )

    smem = pl.BlockSpec(memory_space=pltpu.SMEM)
    vmem = pl.BlockSpec(memory_space=pltpu.VMEM)
    anywhere = pl.BlockSpec(memory_space=pl.ANY)
    params = pltpu.CompilerParams(vmem_limit_bytes=VMEM_LIMIT)
    chunk_flops = 2 * 2 * near * rows * BLK * lanes
    out_shape = jax.ShapeDtypeStruct((1,) + top_trace.shape, jnp.bfloat16)

    def scalars(tick):
        chunk = tick - 2 * layer_pos
        done = jnp.floor_divide(chunk, PARTS) - 1
        valid = jnp.logical_and(done >= 0, done < panel_count)
        bank_pos = assign[layer_pos, jnp.clip(jnp.floor_divide(chunk, PARTS), 0, panel_count - 1)]
        return jnp.stack([bank_pos, jnp.clip(done, 0, panel_count - 1), valid.astype(jnp.int32)]).astype(jnp.int32)

    def exchange(entering):
        if in_pairs:
            near_half = lax.dynamic_slice_in_dim(entering, (1 - is_odd) * (rows - reach_rows), reach_rows)
            far_half = lax.dynamic_slice_in_dim(entering, is_odd * (rows - reach_rows), reach_rows)
            parts = entering[rows:]
            inner = lax.ppermute(
                jnp.concatenate([near_half, parts]), "iface", [(i, i ^ 1) for i in range(iface_count)]
            )
            pair_parts = jnp.concatenate([parts, inner[reach_rows:]])
            outer = lax.ppermute(jnp.concatenate([far_half, pair_parts]), "iface", [(1, 2), (2, 1)])
            edge = lax.ppermute(pair_parts, "iface", [(0, 3), (3, 0)])
            return [inner, outer], (reach_rows, reach_rows), [edge]
        trace = entering[:rows]
        parts = entering[rows : rows + rank].astype(jnp.float32) + entering[rows + rank :].astype(jnp.float32)
        others = lax.psum(parts, "iface") - parts
        distances = [d for d in range(1, reach_shards + 1)]
        halos = [shifted(trace, "iface", d) for d in distances] + [shifted(trace, "iface", -d) for d in distances]
        return halos, (rows,) * len(halos), [others]

    leaving = []
    arrived = None
    stored = None
    for tick in range(tick_count):
        scal = scalars(tick)
        first = top[min(tick, chunk_count - 1)]
        entering = first if tick < 2 else jnp.where(layer_pos == 0, first, arrived)
        arrived = shifted(leaving[tick - 1], "layer", 1) if 0 < tick < tick_count - 1 else None
        halos, halo_rows, sums = exchange(entering)
        with_store = tick >= PARTS and tick % PARTS == 0
        operands = [scal, slot, order, blocks_mat, entering, bank]
        in_specs = [smem, smem, smem, vmem, vmem, anywhere]
        shapes = [jax.ShapeDtypeStruct((rows, lanes), jnp.float32)]
        out_specs = [vmem]
        scratch = [pltpu.VMEM((rows, lanes), jnp.bfloat16), pltpu.VMEM((2, rows, columns), jnp.bfloat16)]
        aliases = {}
        if with_store:
            if stored is None:
                stored = jnp.zeros(out_shape.shape, out_shape.dtype)
            operands += [leaving[tick - 2], leaving[tick - 1], stored]
            in_specs += [vmem, vmem, anywhere]
            shapes.append(out_shape)
            out_specs.append(anywhere)
            scratch.append(pltpu.VMEM((2, rows, columns), jnp.bfloat16))
            aliases = {len(operands) - 1: 1}
        result = pl.pallas_call(
            functools.partial(own_kernel, with_store, early, tick % PARTS),
            out_shape=shapes,
            in_specs=in_specs,
            out_specs=out_specs,
            scratch_shapes=scratch + [pltpu.SemaphoreType.DMA((2,))],
            input_output_aliases=aliases,
            compiler_params=params,
            cost_estimate=pl.CostEstimate(
                flops=chunk_flops * early // near * 256 // lanes, bytes_accessed=4 * rows * columns, transcendentals=0
            ),
            name="own_blocks",
        )(*operands)
        acc = result[0]
        if with_store:
            stored = result[1]
        window_rows = rows + sum(halo_rows)
        updated = pl.pallas_call(
            functools.partial(rest_kernel, early, near, halo_rows, rank),
            out_shape=jax.ShapeDtypeStruct((rows + 2 * rank, lanes), jnp.bfloat16),
            in_specs=[smem, smem] + [vmem] * (5 + len(halos) + len(sums)),
            out_specs=vmem,
            scratch_shapes=[pltpu.VMEM((window_rows, lanes), jnp.bfloat16)] * 2,
            compiler_params=params,
            cost_estimate=pl.CostEstimate(
                flops=chunk_flops * (near - early) // near * 256 // lanes, bytes_accessed=rows * lanes, transcendentals=0
            ),
            name="other_blocks",
        )(slot, order, blocks_mat, acc, entering, left_mat, next_right, *halos, *sums)
        leaving.append(updated)

    return pl.pallas_call(
        store_kernel,
        out_shape=out_shape,
        in_specs=[smem, vmem, vmem, anywhere],
        out_specs=anywhere,
        scratch_shapes=[pltpu.VMEM((2, rows, columns), jnp.bfloat16), pltpu.SemaphoreType.DMA((1,))],
        input_output_aliases={3: 0},
        compiler_params=params,
        name="last_panel",
    )(scalars(tick_count), leaving[-2], leaving[-1], stored)


def solution(mesh):
    return jax.shard_map(
        per_device,
        mesh=mesh,
        in_specs=(
            P("groups", None, "iface", None),
            P("layer", "groups", None, "iface", None),
            P("layer", None, "iface", None, None, None),
            P("iface", None),
            P("layer", None, None, "iface"),
            P("layer", None, None, "iface"),
            P(),
        ),
        out_specs=P("layer", "groups", None, "iface", None),
        check_vma=False,
    )
```

```python
import functools

import jax
import jax.numpy as jnp
from jax import lax
from jax.experimental import pallas as pl
from jax.experimental.pallas import tpu as pltpu
from jax.sharding import PartitionSpec as P

BLK = 256
BAND = 4
PARTS = 2
COST_CUT = 8
VMEM_LIMIT = 6 * 1024 * 1024


def turned(packed):
    half = packed.shape[1] // 2
    return jnp.concatenate([-packed[:, half:], packed[:, :half]], axis=1)


def enter_kernel(rank, panels, top_hbm, right_ref, *rest):
    *top_refs, panel_ref, sem = rest
    _, _, rows, columns = panel_ref.shape
    width = columns // PARTS
    fetches = [
        pltpu.make_async_copy(top_hbm.at[panel], panel_ref.at[at], sem.at[at]) for at, panel in enumerate(panels)
    ]
    for fetch in fetches:
        fetch.start()
    for at, fetch in enumerate(fetches):
        fetch.wait()
        for part in range(PARTS):
            top_ref = top_refs[at * PARTS + part]
            lanes = slice(part * width, (part + 1) * width)
            packed = jnp.concatenate([panel_ref[at, 0, :, lanes], panel_ref[at, 1, :, lanes]], axis=1)
            top_ref[:rows, :] = packed
            both = jnp.dot(right_ref[...], packed, preferred_element_type=jnp.float32)
            put_partial(both, rank, rows, top_ref)


def transpose_kernel(left_ref, out_ref):
    out_ref[...] = left_ref[...].T


def put_partial(both, rank, rows, buffer_ref):
    value = both[:rank] + turned(both[rank:])
    upper = value.astype(jnp.bfloat16)
    buffer_ref[rows : rows + rank, :] = upper
    buffer_ref[rows + rank :, :] = (value - upper.astype(jnp.float32)).astype(jnp.bfloat16)


def near_terms(row, first, last, near, table_ref, blocks_ref, window_ref, turned_ref):
    total = None
    for k in range(first, last):
        start = pl.multiple_of(table_ref[row, k] * BLK, BLK)
        k_pos = table_ref[row, near + k]
        part = jnp.dot(
            blocks_ref[0, row, k_pos], window_ref[pl.ds(start, BLK), :], preferred_element_type=jnp.float32
        )
        part += jnp.dot(
            blocks_ref[1, row, k_pos], turned_ref[pl.ds(start, BLK), :], preferred_element_type=jnp.float32
        )
        total = part if total is None else total + part
    return total


def start_store(table_ref, row, first_ref, second_ref, panel_ref, store):
    rows, half = panel_ref.shape[1], panel_ref.shape[2] // 2

    @pl.when(table_ref[row, 2] == 1)
    def _():
        for comp in range(2):
            lanes = slice(comp * half, (comp + 1) * half)
            panel_ref[comp] = jnp.concatenate([first_ref[:rows, lanes], second_ref[:rows, lanes]], axis=1)
        store.start()


def end_store(table_ref, row, store):
    @pl.when(table_ref[row, 2] == 1)
    def _():
        store.wait()


def own_kernel(tick, early, near, with_store, table_ref, blocks_ref, entering_ref, bank_ref, *rest):
    if with_store:
        first_ref, second_ref = rest[:2]
        acc_ref, window_ref, turned_ref, out_ref, source_ref, panel_ref, sem = rest[-7:]
    elif tick == 0:
        acc_ref, window_ref, turned_ref, _, source_ref, sem, _ = rest
    else:
        acc_ref, window_ref, turned_ref, source_ref, sem = rest
    rows = acc_ref.shape[0]
    half = acc_ref.shape[1] // 2
    if tick == 0:
        blocks_hbm, blocks_ref, hold_sem = blocks_ref, rest[3], rest[-1]
        holds = [
            [pltpu.make_async_copy(blocks_hbm.at[comp, row], blocks_ref.at[comp, row], hold_sem.at[comp, row]) for comp in range(2)]
            for row in range(rows // BLK)
        ]
        for hold in holds[:2]:
            hold[0].start()
            hold[1].start()
    scalars_row = rows // BLK + tick
    fetch = pltpu.make_async_copy(bank_ref.at[table_ref[scalars_row, 0]], source_ref, sem.at[0])
    fetch.start()
    if with_store:
        store = pltpu.make_async_copy(panel_ref, out_ref.at[0, table_ref[scalars_row, 1]], sem.at[1])
        start_store(table_ref, scalars_row, first_ref, second_ref, panel_ref, store)
    window_ref[:rows, :] = entering_ref[:rows, :]
    turned_ref[:rows, :] = turned(entering_ref[:rows, :])
    part = tick % PARTS
    lanes = slice(part * half, (part + 1) * half)

    def add_source(row, value):
        at = slice(row * BLK, (row + 1) * BLK)
        packed = jnp.concatenate([source_ref[0, at, lanes], source_ref[1, at, lanes]], axis=1)
        acc_ref[at, :] = value + packed.astype(jnp.float32)

    waiting = min(2, rows // BLK - 1)
    for row in range(rows // BLK):
        if tick == 0:
            holds[row][0].wait()
            holds[row][1].wait()
            for hold in holds[row + 2 : row + 3]:
                hold[0].start()
                hold[1].start()
        value = near_terms(row, 0, early[row], near, table_ref, blocks_ref, window_ref, turned_ref)
        if value is None:
            value = jnp.zeros((BLK, acc_ref.shape[1]), jnp.float32)
        if row < waiting:
            acc_ref[row * BLK : (row + 1) * BLK, :] = value
            continue
        if row == waiting:
            fetch.wait()
        add_source(row, value)
    for row in range(waiting):
        add_source(row, acc_ref[row * BLK : (row + 1) * BLK, :])
    if with_store:
        end_store(table_ref, scalars_row, store)


def rest_kernel(
    early, near, pieces, parts_at, rank, table_ref, blocks_ref, acc_ref, entering_ref, left_ref, right_ref, *rest
):
    received = rest[:-5]
    leaving_ref, window_ref, turned_ref = rest[-3:]
    rows, lanes = acc_ref.shape
    place = rows
    for source, start, count in pieces:
        value = received[source][start : start + count, :]
        window_ref[place : place + count, :] = value
        turned_ref[place : place + count, :] = turned(value)
        place += count
    coefficient = jnp.zeros((rank, lanes), jnp.float32)
    for ref, start in [(entering_ref, rows)] + [(received[source], start) for source, start in parts_at]:
        for at in range(start, ref.shape[0], rank):
            coefficient += ref[at : at + rank, :].astype(jnp.float32)
    spread = jnp.concatenate([coefficient, turned(coefficient)], axis=0).astype(jnp.bfloat16)
    for row in range(rows // BLK):
        at = slice(row * BLK, (row + 1) * BLK)
        value = jnp.dot(left_ref[at, :], spread, preferred_element_type=jnp.float32)
        if early[row] < near:
            value += near_terms(row, early[row], near, near, table_ref, blocks_ref, window_ref, turned_ref)
        leaving_ref[at, :] = (value + acc_ref[at, :]).astype(jnp.bfloat16)
    both = jnp.dot(right_ref[...], leaving_ref[:rows, :], preferred_element_type=jnp.float32)
    put_partial(both, rank, rows, leaving_ref)


def store_kernel(row, table_ref, first_ref, second_ref, _, out_ref, panel_ref, sem):
    store = pltpu.make_async_copy(panel_ref, out_ref.at[0, table_ref[row, 1]], sem.at[0])
    start_store(table_ref, row, first_ref, second_ref, panel_ref, store)
    end_store(table_ref, row, store)


def in_hbm(array):
    return pltpu.with_memory_space_constraint(array, pltpu.HBM)


def shifted(block, axis, distance):
    devices = range(lax.axis_size(axis))
    route = [(i - distance, i) for i in devices if i - distance in devices]
    return lax.ppermute(block, axis, route)


def down_ring(block):
    count = lax.axis_size("layer")
    return lax.ppermute(block, "layer", [(i, (i + 1) % count) for i in range(count)])


def per_device(top_trace, sources, near_blocks, near_index, far_left, far_right, assign):
    panel_count, _, rows, columns = top_trace.shape
    rank = far_left.shape[2]
    near = near_index.shape[1]
    blocks_dev = rows // BLK
    width = columns // PARTS
    lanes = 2 * width
    reach_rows = BAND * BLK
    reach_shards = -(-reach_rows // rows)
    layer_count = lax.axis_size("layer")
    layer_pos = lax.axis_index("layer")
    iface_count = lax.axis_size("iface")
    iface_pos = lax.axis_index("iface")
    chunk_count = panel_count * PARTS
    tick_count = chunk_count + 2 * (layer_count - 1)
    in_pairs = iface_count == 4 and reach_rows <= rows
    is_odd = iface_pos % 2

    offset = near_index - iface_pos * blocks_dev
    own = jnp.logical_and(offset >= 0, offset < blocks_dev)
    if in_pairs:
        below = jnp.where(is_odd == 1, blocks_dev, blocks_dev + BAND)
        above = jnp.where(is_odd == 1, blocks_dev + BAND, blocks_dev)
        slot = jnp.where(own, offset, jnp.where(offset < 0, below + offset + BAND, above + offset - blocks_dev))
    else:
        shard = jnp.floor_divide(offset, blocks_dev)
        group = jnp.where(shard < 0, -shard, jnp.where(shard > 0, reach_shards + shard, 0))
        slot = group * blocks_dev + offset - shard * blocks_dev
    key = jnp.where(own, 0, near) + jnp.arange(near)[None, :]
    place = jnp.sum(key[:, None, :] < key[:, :, None], axis=2)
    hit = place[:, None, :] == jnp.arange(near)[None, :, None]
    slot = jnp.sum(jnp.where(hit, slot[:, None, :], 0), axis=2).astype(jnp.int32)
    order = jnp.sum(jnp.where(hit, jnp.arange(near)[None, None, :], 0), axis=2).astype(jnp.int32)
    own_offsets = [min(b, BAND) + min(blocks_dev - 1 - b, BAND) + 1 for b in range(blocks_dev)]
    early = tuple(max(0, min(near, count - (2 * BAND + 1 - near))) for count in own_offsets)
    early_flops, late_flops = sum(early), near * blocks_dev - sum(early)

    next_right = shifted(far_right, "layer", -1)[0].reshape(2 * rank, rows)
    bank = in_hbm(sources[0])
    smem = pl.BlockSpec(memory_space=pltpu.SMEM)
    vmem = pl.BlockSpec(memory_space=pltpu.VMEM)
    anywhere = pl.BlockSpec(memory_space=pl.ANY)
    params = pltpu.CompilerParams(vmem_limit_bytes=VMEM_LIMIT)
    buffer_rows = rows + 2 * rank
    own_right = far_right[0].reshape(2 * rank, rows)

    def enter(panels):
        chunks = PARTS * len(panels)
        return pl.pallas_call(
            functools.partial(enter_kernel, rank, panels),
            out_shape=[pltpu.VMEM((buffer_rows, lanes), jnp.bfloat16)] * chunks,
            in_specs=[anywhere, vmem],
            out_specs=[vmem] * chunks,
            scratch_shapes=[
                pltpu.VMEM((len(panels), 2, rows, columns), jnp.bfloat16),
                pltpu.SemaphoreType.DMA((len(panels),)),
            ],
            compiler_params=params,
            name="enter",
        )(in_hbm(top_trace), own_right)

    top = list(enter((0,)))
    left_mat = pl.pallas_call(
        transpose_kernel,
        out_shape=pltpu.VMEM((rows, 2 * rank), jnp.bfloat16),
        in_specs=[vmem],
        out_specs=vmem,
        compiler_params=params,
        name="turn_left",
    )(far_left[0].reshape(2 * rank, rows))
    blocks_mat = in_hbm(near_blocks[0])
    pair_flops = 2 * 2 * BLK * BLK * 256

    table_shape = (tick_count + 1, 2 * near)
    panel = jnp.floor_divide(lax.broadcasted_iota(jnp.int32, table_shape, 0) - 2 * layer_pos, PARTS)
    column = lax.broadcasted_iota(jnp.int32, table_shape, 1)
    held_panel = jnp.clip(panel, 0, panel_count - 1)
    own_layer = lax.broadcasted_iota(jnp.int32, assign.shape, 0) == layer_pos
    own_assign = jnp.sum(jnp.where(own_layer, assign, 0), axis=0)
    each_panel = lax.broadcasted_iota(jnp.int32, (1, 1, panel_count), 2)
    bank_pos = jnp.sum(jnp.where(held_panel[:, :, None] == each_panel, own_assign[None, None, :], 0), axis=2)
    valid = jnp.logical_and(panel >= 1, panel <= panel_count).astype(jnp.int32)
    stored_panel = jnp.clip(panel - 1, 0, panel_count - 1)
    scalars = jnp.where(column == 0, bank_pos, jnp.where(column == 1, stored_panel, valid))
    table = jnp.concatenate([jnp.concatenate([slot, order], axis=1), scalars]).astype(jnp.int32)

    def exchange(entering):
        if in_pairs:
            split = reach_rows // 2
            near_half = lax.dynamic_slice_in_dim(entering, (1 - is_odd) * (rows - reach_rows), reach_rows)
            far_start = is_odd * (rows - reach_rows)
            far_first = lax.dynamic_slice_in_dim(entering, far_start, split)
            far_last = lax.dynamic_slice_in_dim(entering, far_start + split, split)
            parts = entering[rows:]
            swap = [(i, i ^ 1) for i in range(iface_count)]
            inner = lax.ppermute(jnp.concatenate([near_half, far_first, parts]), "iface", swap)
            pair_sum = sum(
                array[at : at + rank].astype(jnp.float32)
                for array in (parts, inner[reach_rows + split :])
                for at in (0, rank)
            )
            upper = lax.reduce_precision(pair_sum, 8, 7)
            is_inner = jnp.logical_or(iface_pos == 1, iface_pos == 2)
            crossing = jnp.concatenate(
                [
                    jnp.where(is_inner, far_last, inner[reach_rows : reach_rows + split]),
                    upper.astype(jnp.bfloat16),
                    (pair_sum - upper).astype(jnp.bfloat16),
                ]
            )
            outer = lax.ppermute(crossing, "iface", [(i, iface_count - 1 - i) for i in range(iface_count)])
            pieces = ((0, 0, reach_rows), (2, 0, split), (1, 0, split))
            return [inner, outer], pieces, ((0, reach_rows + split), (1, split))
        trace = entering[:rows]
        parts = entering[rows : rows + rank].astype(jnp.float32) + entering[rows + rank :].astype(jnp.float32)
        others = lax.psum(parts, "iface") - parts
        distances = [d for d in range(1, reach_shards + 1)]
        halos = [shifted(trace, "iface", d) for d in distances] + [shifted(trace, "iface", -d) for d in distances]
        pieces = tuple((at, 0, rows) for at in range(len(halos)))
        return halos + [others], pieces, ((len(halos), 0),)

    leaving = []
    arrived = None
    stored = None
    for tick in range(tick_count):
        first = top[min(tick, chunk_count - 1)]
        entering = first if tick < 2 else jnp.where(layer_pos == 0, first, arrived)
        arrived = down_ring(updated) if 0 < tick < tick_count - 1 else None
        more, pieces, parts_at = exchange(entering)
        window_rows = rows + sum(count for _, _, count in pieces)
        window = pltpu.VMEM((window_rows, lanes), jnp.bfloat16)
        with_store = tick >= PARTS and tick % PARTS == 0
        operands = [table, blocks_mat, entering, bank]
        in_specs = [smem, anywhere if tick == 0 else vmem, vmem, anywhere]
        shapes = [pltpu.VMEM((rows, lanes), jnp.float32), window, window]
        out_specs = [vmem] * 3
        scratch = [pltpu.VMEM((2, rows, columns), jnp.bfloat16)]
        aliases = {}
        if with_store:
            operands += [leaving[tick - 2], leaving[tick - 1]]
            in_specs += [vmem, vmem]
            if stored is not None:
                aliases = {len(operands): 3}
                operands.append(stored)
                in_specs.append(anywhere)
            shapes.append(pltpu.HBM((1,) + top_trace.shape, jnp.bfloat16))
            out_specs.append(anywhere)
            scratch.append(pltpu.VMEM((2, rows, columns), jnp.bfloat16))
        scratch.append(pltpu.SemaphoreType.DMA((2,)))
        if tick == 0:
            shapes.append(pltpu.VMEM(near_blocks.shape[1:], jnp.bfloat16))
            out_specs.append(vmem)
            scratch.append(pltpu.SemaphoreType.DMA((2, blocks_dev)))
        result = pl.pallas_call(
            functools.partial(own_kernel, tick, early, near, with_store),
            out_shape=shapes,
            in_specs=in_specs,
            out_specs=out_specs,
            scratch_shapes=scratch,
            input_output_aliases=aliases,
            compiler_params=params,
            cost_estimate=pl.CostEstimate(
                flops=pair_flops * early_flops // COST_CUT, bytes_accessed=rows * columns // COST_CUT, transcendentals=0
            ),
            name="own_blocks",
        )(*operands)
        acc, window_own, turned_own = result[:3]
        if tick == 0:
            blocks_mat = result[3]
        if with_store:
            stored = result[3]
        if in_pairs:
            acc, more[-1] = lax.optimization_barrier((acc, more[-1]))
            swap = [(i, i ^ 1) for i in range(iface_count)]
            more.append(lax.ppermute(more[-1][: reach_rows // 2], "iface", swap))
        updated = pl.pallas_call(
            functools.partial(rest_kernel, early, near, pieces, parts_at, rank),
            out_shape=[pltpu.VMEM((buffer_rows, lanes), jnp.bfloat16), window, window],
            in_specs=[smem] + [vmem] * (7 + len(more)),
            out_specs=[vmem] * 3,
            input_output_aliases={6 + len(more): 1, 7 + len(more): 2},
            compiler_params=params,
            cost_estimate=pl.CostEstimate(
                flops=pair_flops * late_flops // COST_CUT, bytes_accessed=rows * lanes // COST_CUT, transcendentals=0
            ),
            name="other_blocks",
        )(table, blocks_mat, acc, entering, left_mat, next_right, *more, window_own, turned_own)[0]
        if tick == 0 and panel_count > 1:
            top += enter(tuple(range(1, panel_count)))
        following = min(tick + 1, chunk_count - 1)
        if arrived is not None:
            kept, arrived, top[following] = lax.optimization_barrier((updated, arrived, top[following]))
        else:
            kept, top[following] = lax.optimization_barrier((updated, top[following]))
        leaving.append(kept)

    return pl.pallas_call(
        functools.partial(store_kernel, blocks_dev + tick_count),
        out_shape=jax.ShapeDtypeStruct((1,) + top_trace.shape, jnp.bfloat16),
        in_specs=[smem, vmem, vmem, anywhere],
        out_specs=anywhere,
        scratch_shapes=[pltpu.VMEM((2, rows, columns), jnp.bfloat16), pltpu.SemaphoreType.DMA((1,))],
        input_output_aliases={3: 0},
        compiler_params=params,
        name="last_panel",
    )(table, leaving[-2], leaving[-1], stored)


def solution(mesh):
    return jax.shard_map(
        per_device,
        mesh=mesh,
        in_specs=(
            P("groups", None, "iface", None),
            P("layer", "groups", None, "iface", None),
            P("layer", None, "iface", None, None, None),
            P("iface", None),
            P("layer", None, None, "iface"),
            P("layer", None, None, "iface"),
            P(),
        ),
        out_specs=P("layer", "groups", None, "iface", None),
        check_vma=False,
    )
```

```python
import functools

import jax
import jax.numpy as jnp
from jax import lax
from jax.experimental import pallas as pl
from jax.experimental.pallas import tpu as pltpu
from jax.sharding import PartitionSpec as P

BLK = 256
BAND = 4
PARTS = 2
COST_CUT = 1000000
VMEM_LIMIT = 6 * 1024 * 1024


def turned(packed):
    half = packed.shape[1] // 2
    return jnp.concatenate([-packed[:, half:], packed[:, :half]], axis=1)


def enter_kernel(rank, panels, top_hbm, right_hbm, *rest):
    *top_refs, panel_ref, right_ref, sem = rest
    _, _, rows, columns = panel_ref.shape
    factor = pltpu.make_async_copy(right_hbm, right_ref, sem.at[len(panels)])
    factor.start()
    width = columns // PARTS
    fetches = [
        pltpu.make_async_copy(top_hbm.at[panel], panel_ref.at[at], sem.at[at]) for at, panel in enumerate(panels)
    ]
    for fetch in fetches:
        fetch.start()
    for at, fetch in enumerate(fetches):
        fetch.wait()
        if at == 0:
            factor.wait()
        for part in range(PARTS):
            top_ref = top_refs[at * PARTS + part]
            lanes = slice(part * width, (part + 1) * width)
            packed = jnp.concatenate([panel_ref[at, 0, :, lanes], panel_ref[at, 1, :, lanes]], axis=1)
            top_ref[:rows, :] = packed
            both = jnp.dot(right_ref[...], packed, preferred_element_type=jnp.float32)
            put_partial(both, rank, rows, top_ref)


def transpose_kernel(left_ref, out_ref):
    out_ref[...] = left_ref[...].T


def put_partial(both, rank, rows, buffer_ref):
    value = both[:rank] + turned(both[rank:])
    upper = value.astype(jnp.bfloat16)
    buffer_ref[rows : rows + rank, :] = upper
    buffer_ref[rows + rank :, :] = (value - upper.astype(jnp.float32)).astype(jnp.bfloat16)


def near_terms(row, first, last, near, table_ref, blocks_ref, window_ref, turned_ref):
    total = None
    for k in range(first, last):
        start = pl.multiple_of(table_ref[row, k] * BLK, BLK)
        k_pos = table_ref[row, near + k]
        part = jnp.dot(
            blocks_ref[0, row, k_pos], window_ref[pl.ds(start, BLK), :], preferred_element_type=jnp.float32
        )
        part += jnp.dot(
            blocks_ref[1, row, k_pos], turned_ref[pl.ds(start, BLK), :], preferred_element_type=jnp.float32
        )
        total = part if total is None else total + part
    return total


def start_store(table_ref, row, first_ref, second_ref, panel_ref, store):
    rows, half = panel_ref.shape[1], panel_ref.shape[2] // 2

    @pl.when(table_ref[row, 2] == 1)
    def _():
        for comp in range(2):
            lanes = slice(comp * half, (comp + 1) * half)
            panel_ref[comp] = jnp.concatenate([first_ref[:rows, lanes], second_ref[:rows, lanes]], axis=1)
        store.start()


def end_store(table_ref, row, store):
    @pl.when(table_ref[row, 2] == 1)
    def _():
        store.wait()


def own_kernel(tick, early, near, with_store, table_ref, blocks_ref, entering_ref, bank_ref, *rest):
    if with_store:
        first_ref, second_ref = rest[:2]
        acc_ref, window_ref, turned_ref, out_ref, source_ref, panel_ref, sem = rest[-7:]
    elif tick == 0:
        acc_ref, window_ref, turned_ref, _, source_ref, sem, _ = rest
    else:
        acc_ref, window_ref, turned_ref, source_ref, sem = rest
    rows = acc_ref.shape[0]
    half = acc_ref.shape[1] // 2
    if tick == 0:
        blocks_hbm, blocks_ref, hold_sem = blocks_ref, rest[3], rest[-1]
        holds = [
            [pltpu.make_async_copy(blocks_hbm.at[comp, row], blocks_ref.at[comp, row], hold_sem.at[comp, row]) for comp in range(2)]
            for row in range(rows // BLK)
        ]
        for hold in holds[:2]:
            hold[0].start()
            hold[1].start()
    scalars_row = rows // BLK + tick
    fetch = pltpu.make_async_copy(bank_ref.at[table_ref[scalars_row, 0]], source_ref, sem.at[0])
    fetch.start()
    if with_store:
        store = pltpu.make_async_copy(panel_ref, out_ref.at[0, table_ref[scalars_row, 1]], sem.at[1])
        start_store(table_ref, scalars_row, first_ref, second_ref, panel_ref, store)
    window_ref[:rows, :] = entering_ref[:rows, :]
    turned_ref[:rows, :] = turned(entering_ref[:rows, :])
    part = tick % PARTS
    lanes = slice(part * half, (part + 1) * half)

    def add_source(row, value):
        at = slice(row * BLK, (row + 1) * BLK)
        packed = jnp.concatenate([source_ref[0, at, lanes], source_ref[1, at, lanes]], axis=1)
        acc_ref[at, :] = value + packed.astype(jnp.float32)

    waiting = min(2, rows // BLK - 1)
    for row in range(rows // BLK):
        if tick == 0:
            holds[row][0].wait()
            holds[row][1].wait()
            for hold in holds[row + 2 : row + 3]:
                hold[0].start()
                hold[1].start()
        value = near_terms(row, 0, early[row], near, table_ref, blocks_ref, window_ref, turned_ref)
        if value is None:
            value = jnp.zeros((BLK, acc_ref.shape[1]), jnp.float32)
        if row < waiting:
            acc_ref[row * BLK : (row + 1) * BLK, :] = value
            continue
        if row == waiting:
            fetch.wait()
        add_source(row, value)
    for row in range(waiting):
        add_source(row, acc_ref[row * BLK : (row + 1) * BLK, :])
    if with_store:
        end_store(table_ref, scalars_row, store)


def rest_kernel(
    early, near, pieces, parts_at, rank, table_ref, blocks_ref, acc_ref, entering_ref, left_ref, right_ref, *rest
):
    received = rest[:-5]
    leaving_ref, window_ref, turned_ref = rest[-3:]
    rows, lanes = acc_ref.shape
    place = rows
    for source, start, count in pieces:
        value = received[source][start : start + count, :]
        window_ref[place : place + count, :] = value
        turned_ref[place : place + count, :] = turned(value)
        place += count
    coefficient = jnp.zeros((rank, lanes), jnp.float32)
    for ref, start in [(entering_ref, rows)] + [(received[source], start) for source, start in parts_at]:
        for at in range(start, ref.shape[0], rank):
            coefficient += ref[at : at + rank, :].astype(jnp.float32)
    spread = jnp.concatenate([coefficient, turned(coefficient)], axis=0).astype(jnp.bfloat16)
    for row in range(rows // BLK):
        at = slice(row * BLK, (row + 1) * BLK)
        value = jnp.dot(left_ref[at, :], spread, preferred_element_type=jnp.float32)
        if early[row] < near:
            value += near_terms(row, early[row], near, near, table_ref, blocks_ref, window_ref, turned_ref)
        leaving_ref[at, :] = (value + acc_ref[at, :]).astype(jnp.bfloat16)
    both = jnp.dot(right_ref[...], leaving_ref[:rows, :], preferred_element_type=jnp.float32)
    put_partial(both, rank, rows, leaving_ref)


def store_kernel(row, table_ref, first_ref, second_ref, _, out_ref, panel_ref, sem):
    store = pltpu.make_async_copy(panel_ref, out_ref.at[0, table_ref[row, 1]], sem.at[0])
    start_store(table_ref, row, first_ref, second_ref, panel_ref, store)
    end_store(table_ref, row, store)


def in_hbm(array):
    return pltpu.with_memory_space_constraint(array, pltpu.HBM)


def shifted(block, axis, distance):
    devices = range(lax.axis_size(axis))
    route = [(i - distance, i) for i in devices if i - distance in devices]
    return lax.ppermute(block, axis, route)


def ring(block, distance):
    count = lax.axis_size("layer")
    return lax.ppermute(block, "layer", [(i, (i + distance) % count) for i in range(count)])


def per_device(top_trace, sources, near_blocks, near_index, far_left, far_right, assign):
    panel_count, _, rows, columns = top_trace.shape
    rank = far_left.shape[2]
    near = near_index.shape[1]
    blocks_dev = rows // BLK
    width = columns // PARTS
    lanes = 2 * width
    reach_rows = BAND * BLK
    reach_shards = -(-reach_rows // rows)
    layer_count = lax.axis_size("layer")
    layer_pos = lax.axis_index("layer")
    iface_count = lax.axis_size("iface")
    iface_pos = lax.axis_index("iface")
    chunk_count = panel_count * PARTS
    tick_count = chunk_count + 2 * (layer_count - 1)
    in_pairs = iface_count == 4 and reach_rows <= rows
    is_odd = iface_pos % 2

    offset = near_index - iface_pos * blocks_dev
    own = jnp.logical_and(offset >= 0, offset < blocks_dev)
    if in_pairs:
        below = jnp.where(is_odd == 1, blocks_dev, blocks_dev + BAND)
        above = jnp.where(is_odd == 1, blocks_dev + BAND, blocks_dev)
        slot = jnp.where(own, offset, jnp.where(offset < 0, below + offset + BAND, above + offset - blocks_dev))
    else:
        shard = jnp.floor_divide(offset, blocks_dev)
        group = jnp.where(shard < 0, -shard, jnp.where(shard > 0, reach_shards + shard, 0))
        slot = group * blocks_dev + offset - shard * blocks_dev
    key = jnp.where(own, 0, near) + jnp.arange(near)[None, :]
    place = jnp.sum(key[:, None, :] < key[:, :, None], axis=2)
    hit = place[:, None, :] == jnp.arange(near)[None, :, None]
    slot = jnp.sum(jnp.where(hit, slot[:, None, :], 0), axis=2).astype(jnp.int32)
    order = jnp.sum(jnp.where(hit, jnp.arange(near)[None, None, :], 0), axis=2).astype(jnp.int32)
    own_offsets = [min(b, BAND) + min(blocks_dev - 1 - b, BAND) + 1 for b in range(blocks_dev)]
    early = tuple(max(0, min(near, count - (2 * BAND + 1 - near))) for count in own_offsets)
    early_flops, late_flops = sum(early), near * blocks_dev - sum(early)

    next_right = ring(far_right, -1)[0].reshape(2 * rank, rows)
    bank = in_hbm(sources[0])
    smem = pl.BlockSpec(memory_space=pltpu.SMEM)
    vmem = pl.BlockSpec(memory_space=pltpu.VMEM)
    anywhere = pl.BlockSpec(memory_space=pl.ANY)
    params = pltpu.CompilerParams(vmem_limit_bytes=VMEM_LIMIT)
    buffer_rows = rows + 2 * rank
    own_right = in_hbm(far_right[0].reshape(2 * rank, rows))

    def enter(panels):
        chunks = PARTS * len(panels)
        return pl.pallas_call(
            functools.partial(enter_kernel, rank, panels),
            out_shape=[pltpu.VMEM((buffer_rows, lanes), jnp.bfloat16)] * chunks,
            in_specs=[anywhere, anywhere],
            out_specs=[vmem] * chunks,
            scratch_shapes=[
                pltpu.VMEM((len(panels), 2, rows, columns), jnp.bfloat16),
                pltpu.VMEM((2 * rank, rows), jnp.bfloat16),
                pltpu.SemaphoreType.DMA((len(panels) + 1,)),
            ],
            compiler_params=params,
            name="enter",
        )(in_hbm(top_trace), own_right)

    top = list(enter((0,)))
    left_mat = pl.pallas_call(
        transpose_kernel,
        out_shape=pltpu.VMEM((rows, 2 * rank), jnp.bfloat16),
        in_specs=[vmem],
        out_specs=vmem,
        compiler_params=params,
        name="turn_left",
    )(far_left[0].reshape(2 * rank, rows))
    blocks_mat = in_hbm(near_blocks[0])
    pair_flops = 2 * 2 * BLK * BLK * 256

    table_shape = (tick_count + 1, 2 * near)
    panel = jnp.floor_divide(lax.broadcasted_iota(jnp.int32, table_shape, 0) - 2 * layer_pos, PARTS)
    column = lax.broadcasted_iota(jnp.int32, table_shape, 1)
    held_panel = jnp.clip(panel, 0, panel_count - 1)
    own_layer = lax.broadcasted_iota(jnp.int32, assign.shape, 0) == layer_pos
    own_assign = jnp.sum(jnp.where(own_layer, assign, 0), axis=0)
    each_panel = lax.broadcasted_iota(jnp.int32, (1, 1, panel_count), 2)
    bank_pos = jnp.sum(jnp.where(held_panel[:, :, None] == each_panel, own_assign[None, None, :], 0), axis=2)
    valid = jnp.logical_and(panel >= 1, panel <= panel_count).astype(jnp.int32)
    stored_panel = jnp.clip(panel - 1, 0, panel_count - 1)
    scalars = jnp.where(column == 0, bank_pos, jnp.where(column == 1, stored_panel, valid))
    table = jnp.concatenate([jnp.concatenate([slot, order], axis=1), scalars]).astype(jnp.int32)
    table, is_first = lax.optimization_barrier((table, layer_pos == 0))

    def exchange(entering):
        if in_pairs:
            split = reach_rows // 2
            near_half = lax.dynamic_slice_in_dim(entering, (1 - is_odd) * (rows - reach_rows), reach_rows)
            far_start = is_odd * (rows - reach_rows)
            far_first = lax.dynamic_slice_in_dim(entering, far_start, split)
            far_last = lax.dynamic_slice_in_dim(entering, far_start + split, split)
            parts = entering[rows:]
            swap = [(i, i ^ 1) for i in range(iface_count)]
            inner = lax.ppermute(jnp.concatenate([near_half, far_first, parts]), "iface", swap)
            pair_sum = sum(
                array[at : at + rank].astype(jnp.float32)
                for array in (parts, inner[reach_rows + split :])
                for at in (0, rank)
            )
            upper = lax.reduce_precision(pair_sum, 8, 7)
            is_inner = jnp.logical_or(iface_pos == 1, iface_pos == 2)
            crossing = jnp.concatenate(
                [
                    jnp.where(is_inner, far_last, inner[reach_rows : reach_rows + split]),
                    upper.astype(jnp.bfloat16),
                    (pair_sum - upper).astype(jnp.bfloat16),
                ]
            )
            outer = lax.ppermute(crossing, "iface", [(i, iface_count - 1 - i) for i in range(iface_count)])
            pieces = ((0, 0, reach_rows), (2, 0, split), (1, 0, split))
            return [inner, outer], pieces, ((0, reach_rows + split), (1, split))
        trace = entering[:rows]
        parts = entering[rows : rows + rank].astype(jnp.float32) + entering[rows + rank :].astype(jnp.float32)
        others = lax.psum(parts, "iface") - parts
        distances = [d for d in range(1, reach_shards + 1)]
        halos = [shifted(trace, "iface", d) for d in distances] + [shifted(trace, "iface", -d) for d in distances]
        pieces = tuple((at, 0, rows) for at in range(len(halos)))
        return halos + [others], pieces, ((len(halos), 0),)

    leaving = []
    arrived = None
    stored = None
    for tick in range(tick_count):
        first = top[min(tick, chunk_count - 1)]
        entering = first if tick < 2 else jnp.where(is_first, first, arrived)
        arrived = ring(updated, 1) if 0 < tick < tick_count - 1 else None
        more, pieces, parts_at = exchange(entering)
        window_rows = rows + sum(count for _, _, count in pieces)
        window = pltpu.VMEM((window_rows, lanes), jnp.bfloat16)
        with_store = tick >= PARTS and tick % PARTS == 0
        operands = [table, blocks_mat, entering, bank]
        in_specs = [smem, anywhere if tick == 0 else vmem, vmem, anywhere]
        shapes = [pltpu.VMEM((rows, lanes), jnp.float32), window, window]
        out_specs = [vmem] * 3
        scratch = [pltpu.VMEM((2, rows, columns), jnp.bfloat16)]
        aliases = {}
        if with_store:
            operands += [leaving[tick - 2], leaving[tick - 1]]
            in_specs += [vmem, vmem]
            if stored is not None:
                aliases = {len(operands): 3}
                operands.append(stored)
                in_specs.append(anywhere)
            shapes.append(pltpu.HBM((1,) + top_trace.shape, jnp.bfloat16))
            out_specs.append(anywhere)
            scratch.append(pltpu.VMEM((2, rows, columns), jnp.bfloat16))
        scratch.append(pltpu.SemaphoreType.DMA((2,)))
        if tick == 0:
            shapes.append(pltpu.VMEM(near_blocks.shape[1:], jnp.bfloat16))
            out_specs.append(vmem)
            scratch.append(pltpu.SemaphoreType.DMA((2, blocks_dev)))
        result = pl.pallas_call(
            functools.partial(own_kernel, tick, early, near, with_store),
            out_shape=shapes,
            in_specs=in_specs,
            out_specs=out_specs,
            scratch_shapes=scratch,
            input_output_aliases=aliases,
            compiler_params=params,
            cost_estimate=pl.CostEstimate(
                flops=pair_flops * early_flops // COST_CUT, bytes_accessed=rows * columns // COST_CUT, transcendentals=0
            ),
            name="own_blocks",
        )(*operands)
        acc, window_own, turned_own = result[:3]
        if tick == 0:
            blocks_mat = result[3]
        if with_store:
            stored = result[3]
        if in_pairs:
            acc, more[-1] = lax.optimization_barrier((acc, more[-1]))
            swap = [(i, i ^ 1) for i in range(iface_count)]
            more.append(lax.ppermute(more[-1][: reach_rows // 2], "iface", swap))
        updated = pl.pallas_call(
            functools.partial(rest_kernel, early, near, pieces, parts_at, rank),
            out_shape=[pltpu.VMEM((buffer_rows, lanes), jnp.bfloat16), window, window],
            in_specs=[smem] + [vmem] * (7 + len(more)),
            out_specs=[vmem] * 3,
            input_output_aliases={6 + len(more): 1, 7 + len(more): 2},
            compiler_params=params,
            cost_estimate=pl.CostEstimate(
                flops=pair_flops * late_flops // COST_CUT, bytes_accessed=rows * lanes // COST_CUT, transcendentals=0
            ),
            name="other_blocks",
        )(table, blocks_mat, acc, entering, left_mat, next_right, *more, window_own, turned_own)[0]
        if tick == 0 and panel_count > 1:
            top += enter(tuple(range(1, panel_count)))
        following = min(tick + 1, chunk_count - 1)
        if arrived is not None:
            kept, arrived, top[following] = lax.optimization_barrier((updated, arrived, top[following]))
        else:
            kept, top[following] = lax.optimization_barrier((updated, top[following]))
        leaving.append(kept)

    return pl.pallas_call(
        functools.partial(store_kernel, blocks_dev + tick_count),
        out_shape=jax.ShapeDtypeStruct((1,) + top_trace.shape, jnp.bfloat16),
        in_specs=[smem, vmem, vmem, anywhere],
        out_specs=anywhere,
        scratch_shapes=[pltpu.VMEM((2, rows, columns), jnp.bfloat16), pltpu.SemaphoreType.DMA((1,))],
        input_output_aliases={3: 0},
        compiler_params=params,
        name="last_panel",
    )(table, leaving[-2], leaving[-1], stored)


def solution(mesh):
    return jax.shard_map(
        per_device,
        mesh=mesh,
        in_specs=(
            P("groups", None, "iface", None),
            P("layer", "groups", None, "iface", None),
            P("layer", None, "iface", None, None, None),
            P("iface", None),
            P("layer", None, None, "iface"),
            P("layer", None, None, "iface"),
            P(),
        ),
        out_specs=P("layer", "groups", None, "iface", None),
        check_vma=False,
    )
```

```python
import functools

import jax
import jax.numpy as jnp
from jax import lax
from jax.experimental import pallas as pl
from jax.experimental.pallas import tpu as pltpu
from jax.sharding import PartitionSpec as P

BLK = 256
BAND = 4
PARTS = 2
COST_CUT = 1000000
VMEM_LIMIT = 6 * 1024 * 1024


def turned(packed):
    half = packed.shape[1] // 2
    return jnp.concatenate([-packed[:, half:], packed[:, :half]], axis=1)


def enter_kernel(rank, panels, top_hbm, right_hbm, *rest):
    *top_refs, panel_ref, right_ref, sem = rest
    _, _, rows, columns = panel_ref.shape
    factor = pltpu.make_async_copy(right_hbm, right_ref, sem.at[len(panels)])
    factor.start()
    width = columns // PARTS
    fetches = [
        pltpu.make_async_copy(top_hbm.at[panel], panel_ref.at[at], sem.at[at]) for at, panel in enumerate(panels)
    ]
    for fetch in fetches:
        fetch.start()
    for at, fetch in enumerate(fetches):
        fetch.wait()
        if at == 0:
            factor.wait()
        for part in range(PARTS):
            top_ref = top_refs[at * PARTS + part]
            lanes = slice(part * width, (part + 1) * width)
            packed = jnp.concatenate([panel_ref[at, 0, :, lanes], panel_ref[at, 1, :, lanes]], axis=1)
            top_ref[:rows, :] = packed
            both = jnp.dot(right_ref[...], packed, preferred_element_type=jnp.float32)
            put_partial(both, rank, rows, top_ref)


def transpose_kernel(left_ref, out_ref):
    out_ref[...] = left_ref[...].T


def put_partial(both, rank, rows, buffer_ref):
    value = both[:rank] + turned(both[rank:])
    buffer_ref[rows : rows + rank, :] = value.astype(jnp.bfloat16)


def near_terms(row, first, last, near, table_ref, blocks_ref, window_ref, turned_ref):
    total = None
    for k in range(first, last):
        start = pl.multiple_of(table_ref[row, k] * BLK, BLK)
        k_pos = table_ref[row, near + k]
        part = jnp.dot(
            blocks_ref[0, row, k_pos], window_ref[pl.ds(start, BLK), :], preferred_element_type=jnp.float32
        )
        part += jnp.dot(
            blocks_ref[1, row, k_pos], turned_ref[pl.ds(start, BLK), :], preferred_element_type=jnp.float32
        )
        total = part if total is None else total + part
    return total


def start_store(table_ref, row, first_ref, second_ref, panel_ref, store):
    rows, half = panel_ref.shape[1], panel_ref.shape[2] // 2

    @pl.when(table_ref[row, 2] == 1)
    def _():
        for comp in range(2):
            lanes = slice(comp * half, (comp + 1) * half)
            panel_ref[comp] = jnp.concatenate([first_ref[:rows, lanes], second_ref[:rows, lanes]], axis=1)
        store.start()


def end_store(table_ref, row, store):
    @pl.when(table_ref[row, 2] == 1)
    def _():
        store.wait()


def own_kernel(tick, early, near, with_store, table_ref, blocks_ref, entering_ref, bank_ref, *rest):
    if with_store:
        first_ref, second_ref = rest[:2]
        acc_ref, window_ref, turned_ref, out_ref, source_ref, panel_ref, sem = rest[-7:]
    elif tick == 0:
        acc_ref, window_ref, turned_ref, _, source_ref, sem, _ = rest
    else:
        acc_ref, window_ref, turned_ref, source_ref, sem = rest
    rows = acc_ref.shape[0]
    half = acc_ref.shape[1] // 2
    if tick == 0:
        blocks_hbm, blocks_ref, hold_sem = blocks_ref, rest[3], rest[-1]
        holds = [
            [pltpu.make_async_copy(blocks_hbm.at[comp, row], blocks_ref.at[comp, row], hold_sem.at[comp, row]) for comp in range(2)]
            for row in range(rows // BLK)
        ]
        for hold in holds[:2]:
            hold[0].start()
            hold[1].start()
    scalars_row = rows // BLK + tick
    fetch = pltpu.make_async_copy(bank_ref.at[table_ref[scalars_row, 0]], source_ref, sem.at[0])
    fetch.start()
    if with_store:
        store = pltpu.make_async_copy(panel_ref, out_ref.at[0, table_ref[scalars_row, 1]], sem.at[1])
        start_store(table_ref, scalars_row, first_ref, second_ref, panel_ref, store)
    window_ref[:rows, :] = entering_ref[:rows, :]
    turned_ref[:rows, :] = turned(entering_ref[:rows, :])
    part = tick % PARTS
    lanes = slice(part * half, (part + 1) * half)

    def add_source(row, value):
        at = slice(row * BLK, (row + 1) * BLK)
        packed = jnp.concatenate([source_ref[0, at, lanes], source_ref[1, at, lanes]], axis=1)
        acc_ref[at, :] = value + packed.astype(jnp.float32)

    waiting = min(2, rows // BLK - 1)
    for row in range(rows // BLK):
        if tick == 0:
            holds[row][0].wait()
            holds[row][1].wait()
            for hold in holds[row + 2 : row + 3]:
                hold[0].start()
                hold[1].start()
        value = near_terms(row, 0, early[row], near, table_ref, blocks_ref, window_ref, turned_ref)
        if value is None:
            value = jnp.zeros((BLK, acc_ref.shape[1]), jnp.float32)
        if row < waiting:
            acc_ref[row * BLK : (row + 1) * BLK, :] = value
            continue
        if row == waiting:
            fetch.wait()
        add_source(row, value)
    for row in range(waiting):
        add_source(row, acc_ref[row * BLK : (row + 1) * BLK, :])
    if with_store:
        end_store(table_ref, scalars_row, store)


def rest_kernel(
    early, near, pieces, parts_at, rank, table_ref, blocks_ref, acc_ref, entering_ref, left_ref, right_ref, *rest
):
    received = rest[:-5]
    leaving_ref, window_ref, turned_ref = rest[-3:]
    rows, lanes = acc_ref.shape
    place = rows
    for source, start, count in pieces:
        value = received[source][start : start + count, :]
        window_ref[place : place + count, :] = value
        turned_ref[place : place + count, :] = turned(value)
        place += count
    coefficient = jnp.zeros((rank, lanes), jnp.float32)
    for ref, start in [(entering_ref, rows)] + [(received[source], start) for source, start in parts_at]:
        for at in range(start, ref.shape[0], rank):
            coefficient += ref[at : at + rank, :].astype(jnp.float32)
    spread = jnp.concatenate([coefficient, turned(coefficient)], axis=0).astype(jnp.bfloat16)
    for row in range(rows // BLK):
        at = slice(row * BLK, (row + 1) * BLK)
        value = jnp.dot(left_ref[at, :], spread, preferred_element_type=jnp.float32)
        if early[row] < near:
            value += near_terms(row, early[row], near, near, table_ref, blocks_ref, window_ref, turned_ref)
        leaving_ref[at, :] = (value + acc_ref[at, :]).astype(jnp.bfloat16)
    both = jnp.dot(right_ref[...], leaving_ref[:rows, :], preferred_element_type=jnp.float32)
    put_partial(both, rank, rows, leaving_ref)


def store_kernel(row, table_ref, first_ref, second_ref, _, out_ref, panel_ref, sem):
    store = pltpu.make_async_copy(panel_ref, out_ref.at[0, table_ref[row, 1]], sem.at[0])
    start_store(table_ref, row, first_ref, second_ref, panel_ref, store)
    end_store(table_ref, row, store)


def in_hbm(array):
    return pltpu.with_memory_space_constraint(array, pltpu.HBM)


def shifted(block, axis, distance):
    devices = range(lax.axis_size(axis))
    route = [(i - distance, i) for i in devices if i - distance in devices]
    return lax.ppermute(block, axis, route)


def ring(block, distance):
    count = lax.axis_size("layer")
    return lax.ppermute(block, "layer", [(i, (i + distance) % count) for i in range(count)])


def per_device(top_trace, sources, near_blocks, near_index, far_left, far_right, assign):
    panel_count, _, rows, columns = top_trace.shape
    rank = far_left.shape[2]
    near = near_index.shape[1]
    blocks_dev = rows // BLK
    width = columns // PARTS
    lanes = 2 * width
    reach_rows = BAND * BLK
    reach_shards = -(-reach_rows // rows)
    layer_count = lax.axis_size("layer")
    layer_pos = lax.axis_index("layer")
    iface_count = lax.axis_size("iface")
    iface_pos = lax.axis_index("iface")
    chunk_count = panel_count * PARTS
    tick_count = chunk_count + 2 * (layer_count - 1)
    in_pairs = iface_count == 4 and reach_rows <= rows
    is_odd = iface_pos % 2

    offset = near_index - iface_pos * blocks_dev
    own = jnp.logical_and(offset >= 0, offset < blocks_dev)
    if in_pairs:
        below = jnp.where(is_odd == 1, blocks_dev, blocks_dev + BAND)
        above = jnp.where(is_odd == 1, blocks_dev + BAND, blocks_dev)
        slot = jnp.where(own, offset, jnp.where(offset < 0, below + offset + BAND, above + offset - blocks_dev))
    else:
        shard = jnp.floor_divide(offset, blocks_dev)
        group = jnp.where(shard < 0, -shard, jnp.where(shard > 0, reach_shards + shard, 0))
        slot = group * blocks_dev + offset - shard * blocks_dev
    key = jnp.where(own, 0, near) + jnp.arange(near)[None, :]
    place = jnp.sum(key[:, None, :] < key[:, :, None], axis=2)
    hit = place[:, None, :] == jnp.arange(near)[None, :, None]
    slot = jnp.sum(jnp.where(hit, slot[:, None, :], 0), axis=2).astype(jnp.int32)
    order = jnp.sum(jnp.where(hit, jnp.arange(near)[None, None, :], 0), axis=2).astype(jnp.int32)
    own_offsets = [min(b, BAND) + min(blocks_dev - 1 - b, BAND) + 1 for b in range(blocks_dev)]
    early = tuple(max(0, min(near, count - (2 * BAND + 1 - near))) for count in own_offsets)
    early_flops, late_flops = sum(early), near * blocks_dev - sum(early)

    next_right = ring(far_right, -1)[0].reshape(2 * rank, rows)
    bank = in_hbm(sources[0])
    smem = pl.BlockSpec(memory_space=pltpu.SMEM)
    vmem = pl.BlockSpec(memory_space=pltpu.VMEM)
    anywhere = pl.BlockSpec(memory_space=pl.ANY)
    params = pltpu.CompilerParams(vmem_limit_bytes=VMEM_LIMIT)
    buffer_rows = rows + rank
    own_right = in_hbm(far_right[0].reshape(2 * rank, rows))

    def enter(panels):
        chunks = PARTS * len(panels)
        return pl.pallas_call(
            functools.partial(enter_kernel, rank, panels),
            out_shape=[pltpu.VMEM((buffer_rows, lanes), jnp.bfloat16)] * chunks,
            in_specs=[anywhere, anywhere],
            out_specs=[vmem] * chunks,
            scratch_shapes=[
                pltpu.VMEM((len(panels), 2, rows, columns), jnp.bfloat16),
                pltpu.VMEM((2 * rank, rows), jnp.bfloat16),
                pltpu.SemaphoreType.DMA((len(panels) + 1,)),
            ],
            compiler_params=params,
            name="enter",
        )(in_hbm(top_trace), own_right)

    top = list(enter((0,)))
    left_mat = pl.pallas_call(
        transpose_kernel,
        out_shape=pltpu.VMEM((rows, 2 * rank), jnp.bfloat16),
        in_specs=[vmem],
        out_specs=vmem,
        compiler_params=params,
        name="turn_left",
    )(far_left[0].reshape(2 * rank, rows))
    blocks_mat = in_hbm(near_blocks[0])
    pair_flops = 2 * 2 * BLK * BLK * 256

    table_shape = (tick_count + 1, 2 * near)
    panel = jnp.floor_divide(lax.broadcasted_iota(jnp.int32, table_shape, 0) - 2 * layer_pos, PARTS)
    column = lax.broadcasted_iota(jnp.int32, table_shape, 1)
    held_panel = jnp.clip(panel, 0, panel_count - 1)
    own_layer = lax.broadcasted_iota(jnp.int32, assign.shape, 0) == layer_pos
    own_assign = jnp.sum(jnp.where(own_layer, assign, 0), axis=0)
    each_panel = lax.broadcasted_iota(jnp.int32, (1, 1, panel_count), 2)
    bank_pos = jnp.sum(jnp.where(held_panel[:, :, None] == each_panel, own_assign[None, None, :], 0), axis=2)
    valid = jnp.logical_and(panel >= 1, panel <= panel_count).astype(jnp.int32)
    stored_panel = jnp.clip(panel - 1, 0, panel_count - 1)
    scalars = jnp.where(column == 0, bank_pos, jnp.where(column == 1, stored_panel, valid))
    table = jnp.concatenate([jnp.concatenate([slot, order], axis=1), scalars]).astype(jnp.int32)
    table, is_first = lax.optimization_barrier((table, layer_pos == 0))

    def exchange(entering):
        if in_pairs:
            split = reach_rows // 2
            near_half = lax.dynamic_slice_in_dim(entering, (1 - is_odd) * (rows - reach_rows), reach_rows)
            far_start = is_odd * (rows - reach_rows)
            far_first = lax.dynamic_slice_in_dim(entering, far_start, split)
            far_last = lax.dynamic_slice_in_dim(entering, far_start + split, split)
            parts = entering[rows:]
            swap = [(i, i ^ 1) for i in range(iface_count)]
            inner = lax.ppermute(jnp.concatenate([near_half, far_first, parts]), "iface", swap)
            pair_sum = parts.astype(jnp.float32) + inner[reach_rows + split :].astype(jnp.float32)
            is_inner = jnp.logical_or(iface_pos == 1, iface_pos == 2)
            crossing = jnp.concatenate(
                [
                    jnp.where(is_inner, far_last, inner[reach_rows : reach_rows + split]),
                    pair_sum.astype(jnp.bfloat16),
                ]
            )
            outer = lax.ppermute(crossing, "iface", [(i, iface_count - 1 - i) for i in range(iface_count)])
            pieces = ((0, 0, reach_rows), (2, 0, split), (1, 0, split))
            return [inner, outer], pieces, ((0, reach_rows + split), (1, split))
        trace = entering[:rows]
        parts = entering[rows:].astype(jnp.float32)
        others = lax.psum(parts, "iface") - parts
        distances = [d for d in range(1, reach_shards + 1)]
        halos = [shifted(trace, "iface", d) for d in distances] + [shifted(trace, "iface", -d) for d in distances]
        pieces = tuple((at, 0, rows) for at in range(len(halos)))
        return halos + [others], pieces, ((len(halos), 0),)

    leaving = []
    arrived = None
    stored = None
    for tick in range(tick_count):
        first = top[min(tick, chunk_count - 1)]
        entering = first if tick < 2 else jnp.where(is_first, first, arrived)
        arrived = shifted(updated, "layer", 1) if 0 < tick < tick_count - 1 else None
        more, pieces, parts_at = exchange(entering)
        window_rows = rows + sum(count for _, _, count in pieces)
        window = pltpu.VMEM((window_rows, lanes), jnp.bfloat16)
        with_store = tick >= PARTS and tick % PARTS == 0
        operands = [table, blocks_mat, entering, bank]
        in_specs = [smem, anywhere if tick == 0 else vmem, vmem, anywhere]
        shapes = [pltpu.VMEM((rows, lanes), jnp.float32), window, window]
        out_specs = [vmem] * 3
        scratch = [pltpu.VMEM((2, rows, columns), jnp.bfloat16)]
        aliases = {}
        if with_store:
            operands += [leaving[tick - 2], leaving[tick - 1]]
            in_specs += [vmem, vmem]
            if stored is not None:
                aliases = {len(operands): 3}
                operands.append(stored)
                in_specs.append(anywhere)
            shapes.append(pltpu.HBM((1,) + top_trace.shape, jnp.bfloat16))
            out_specs.append(anywhere)
            scratch.append(pltpu.VMEM((2, rows, columns), jnp.bfloat16))
        scratch.append(pltpu.SemaphoreType.DMA((2,)))
        if tick == 0:
            shapes.append(pltpu.VMEM(near_blocks.shape[1:], jnp.bfloat16))
            out_specs.append(vmem)
            scratch.append(pltpu.SemaphoreType.DMA((2, blocks_dev)))
        result = pl.pallas_call(
            functools.partial(own_kernel, tick, early, near, with_store),
            out_shape=shapes,
            in_specs=in_specs,
            out_specs=out_specs,
            scratch_shapes=scratch,
            input_output_aliases=aliases,
            compiler_params=params,
            cost_estimate=pl.CostEstimate(
                flops=pair_flops * early_flops // COST_CUT, bytes_accessed=rows * columns // COST_CUT, transcendentals=0
            ),
            name="own_blocks",
        )(*operands)
        acc, window_own, turned_own = result[:3]
        if tick == 0:
            blocks_mat = result[3]
        if with_store:
            stored = result[3]
        if in_pairs:
            acc, more[-1] = lax.optimization_barrier((acc, more[-1]))
            swap = [(i, i ^ 1) for i in range(iface_count)]
            more.append(lax.ppermute(more[-1][: reach_rows // 2], "iface", swap))
        updated = pl.pallas_call(
            functools.partial(rest_kernel, early, near, pieces, parts_at, rank),
            out_shape=[pltpu.VMEM((buffer_rows, lanes), jnp.bfloat16), window, window],
            in_specs=[smem] + [vmem] * (7 + len(more)),
            out_specs=[vmem] * 3,
            input_output_aliases={6 + len(more): 1, 7 + len(more): 2},
            compiler_params=params,
            cost_estimate=pl.CostEstimate(
                flops=pair_flops * late_flops // COST_CUT, bytes_accessed=rows * lanes // COST_CUT, transcendentals=0
            ),
            name="other_blocks",
        )(table, blocks_mat, acc, entering, left_mat, next_right, *more, window_own, turned_own)[0]
        if tick == 0 and panel_count > 1:
            top += enter(tuple(range(1, panel_count)))
        following = min(tick + 1, chunk_count - 1)
        if arrived is not None:
            kept, arrived, top[following] = lax.optimization_barrier((updated, arrived, top[following]))
        else:
            kept, top[following] = lax.optimization_barrier((updated, top[following]))
        leaving.append(kept)

    return pl.pallas_call(
        functools.partial(store_kernel, blocks_dev + tick_count),
        out_shape=jax.ShapeDtypeStruct((1,) + top_trace.shape, jnp.bfloat16),
        in_specs=[smem, vmem, vmem, anywhere],
        out_specs=anywhere,
        scratch_shapes=[pltpu.VMEM((2, rows, columns), jnp.bfloat16), pltpu.SemaphoreType.DMA((1,))],
        input_output_aliases={3: 0},
        compiler_params=params,
        name="last_panel",
    )(table, leaving[-2], leaving[-1], stored)


def solution(mesh):
    return jax.shard_map(
        per_device,
        mesh=mesh,
        in_specs=(
            P("groups", None, "iface", None),
            P("layer", "groups", None, "iface", None),
            P("layer", None, "iface", None, None, None),
            P("iface", None),
            P("layer", None, None, "iface"),
            P("layer", None, None, "iface"),
            P(),
        ),
        out_specs=P("layer", "groups", None, "iface", None),
        check_vma=False,
    )
```

```python
import functools

import jax
import jax.numpy as jnp
from jax import lax
from jax.experimental import pallas as pl
from jax.experimental.pallas import tpu as pltpu
from jax.sharding import PartitionSpec as P

BLK = 256
BAND = 4
PARTS = 2
COST_CUT = 1000000
VMEM_LIMIT = 6 * 1024 * 1024


def turned(packed):
    half = packed.shape[1] // 2
    return jnp.concatenate([-packed[:, half:], packed[:, :half]], axis=1)


def enter_kernel(rank, panels, top_hbm, right_hbm, *rest):
    *top_refs, panel_ref, right_ref, sem = rest
    _, _, rows, columns = panel_ref.shape
    factor = pltpu.make_async_copy(right_hbm, right_ref, sem.at[len(panels)])
    factor.start()
    width = columns // PARTS
    fetches = [
        pltpu.make_async_copy(top_hbm.at[panel], panel_ref.at[at], sem.at[at]) for at, panel in enumerate(panels)
    ]
    for fetch in fetches:
        fetch.start()
    for at, fetch in enumerate(fetches):
        fetch.wait()
        if at == 0:
            factor.wait()
        for part in range(PARTS):
            top_ref = top_refs[at * PARTS + part]
            lanes = slice(part * width, (part + 1) * width)
            packed = jnp.concatenate([panel_ref[at, 0, :, lanes], panel_ref[at, 1, :, lanes]], axis=1)
            top_ref[:rows, :] = packed
            both = jnp.dot(right_ref[...], packed, preferred_element_type=jnp.float32)
            put_partial(both, rank, rows, top_ref)


def transpose_kernel(left_ref, out_ref):
    out_ref[...] = left_ref[...].T


def put_partial(both, rank, rows, buffer_ref):
    value = both[:rank] + turned(both[rank:])
    buffer_ref[rows : rows + rank, :] = value.astype(jnp.bfloat16)


def near_terms(row, first, last, near, table_ref, blocks_ref, window_ref, turned_ref):
    total = None
    for k in range(first, last):
        start = pl.multiple_of(table_ref[row, k] * BLK, BLK)
        k_pos = table_ref[row, near + k]
        part = jnp.dot(
            blocks_ref[0, row, k_pos], window_ref[pl.ds(start, BLK), :], preferred_element_type=jnp.float32
        )
        part += jnp.dot(
            blocks_ref[1, row, k_pos], turned_ref[pl.ds(start, BLK), :], preferred_element_type=jnp.float32
        )
        total = part if total is None else total + part
    return total


def start_store(table_ref, row, first_ref, second_ref, panel_ref, store):
    rows, half = panel_ref.shape[1], panel_ref.shape[2] // 2

    @pl.when(table_ref[row, 2] == 1)
    def _():
        for comp in range(2):
            lanes = slice(comp * half, (comp + 1) * half)
            panel_ref[comp] = jnp.concatenate([first_ref[:rows, lanes], second_ref[:rows, lanes]], axis=1)
        store.start()


def end_store(table_ref, row, store):
    @pl.when(table_ref[row, 2] == 1)
    def _():
        store.wait()


def own_kernel(tick, early, near, with_store, table_ref, blocks_ref, entering_ref, bank_ref, *rest):
    if with_store:
        first_ref, second_ref = rest[:2]
        acc_ref, window_ref, turned_ref, out_ref, source_ref, panel_ref, sem = rest[-7:]
    elif tick == 0:
        acc_ref, window_ref, turned_ref, _, source_ref, sem, _ = rest
    else:
        acc_ref, window_ref, turned_ref, source_ref, sem = rest
    rows = acc_ref.shape[0]
    half = acc_ref.shape[1] // 2
    if tick == 0:
        blocks_hbm, blocks_ref, hold_sem = blocks_ref, rest[3], rest[-1]
        holds = [
            [pltpu.make_async_copy(blocks_hbm.at[comp, row], blocks_ref.at[comp, row], hold_sem.at[comp, row]) for comp in range(2)]
            for row in range(rows // BLK)
        ]
        for hold in holds[:4]:
            hold[0].start()
            hold[1].start()
    scalars_row = rows // BLK + tick
    fetch = pltpu.make_async_copy(bank_ref.at[table_ref[scalars_row, 0]], source_ref, sem.at[0])
    fetch.start()
    if with_store:
        store = pltpu.make_async_copy(panel_ref, out_ref.at[0, table_ref[scalars_row, 1]], sem.at[1])
        start_store(table_ref, scalars_row, first_ref, second_ref, panel_ref, store)
    window_ref[:rows, :] = entering_ref[:rows, :]
    turned_ref[:rows, :] = turned(entering_ref[:rows, :])
    part = tick % PARTS
    lanes = slice(part * half, (part + 1) * half)

    def add_source(row, value):
        at = slice(row * BLK, (row + 1) * BLK)
        packed = jnp.concatenate([source_ref[0, at, lanes], source_ref[1, at, lanes]], axis=1)
        acc_ref[at, :] = value + packed.astype(jnp.float32)

    waiting = min(2, rows // BLK - 1)
    for row in range(rows // BLK):
        if tick == 0:
            holds[row][0].wait()
            holds[row][1].wait()
            for hold in holds[row + 4 : row + 5]:
                hold[0].start()
                hold[1].start()
        value = near_terms(row, 0, early[row], near, table_ref, blocks_ref, window_ref, turned_ref)
        if value is None:
            value = jnp.zeros((BLK, acc_ref.shape[1]), jnp.float32)
        if row < waiting:
            acc_ref[row * BLK : (row + 1) * BLK, :] = value
            continue
        if row == waiting:
            fetch.wait()
        add_source(row, value)
    for row in range(waiting):
        add_source(row, acc_ref[row * BLK : (row + 1) * BLK, :])
    if with_store:
        end_store(table_ref, scalars_row, store)


def rest_kernel(
    early, near, pieces, parts_at, rank, table_ref, blocks_ref, acc_ref, entering_ref, left_ref, right_ref, *rest
):
    received = rest[:-5]
    leaving_ref, window_ref, turned_ref = rest[-3:]
    rows, lanes = acc_ref.shape
    place = rows
    for source, start, count in pieces:
        value = received[source][start : start + count, :]
        window_ref[place : place + count, :] = value
        turned_ref[place : place + count, :] = turned(value)
        place += count
    coefficient = jnp.zeros((rank, lanes), jnp.float32)
    for ref, start in [(entering_ref, rows)] + [(received[source], start) for source, start in parts_at]:
        for at in range(start, ref.shape[0], rank):
            coefficient += ref[at : at + rank, :].astype(jnp.float32)
    spread = jnp.concatenate([coefficient, turned(coefficient)], axis=0).astype(jnp.bfloat16)
    for row in range(rows // BLK):
        at = slice(row * BLK, (row + 1) * BLK)
        value = jnp.dot(left_ref[at, :], spread, preferred_element_type=jnp.float32)
        if early[row] < near:
            value += near_terms(row, early[row], near, near, table_ref, blocks_ref, window_ref, turned_ref)
        leaving_ref[at, :] = (value + acc_ref[at, :]).astype(jnp.bfloat16)
    both = jnp.dot(right_ref[...], leaving_ref[:rows, :], preferred_element_type=jnp.float32)
    put_partial(both, rank, rows, leaving_ref)


def store_kernel(row, table_ref, first_ref, second_ref, _, out_ref, panel_ref, sem):
    store = pltpu.make_async_copy(panel_ref, out_ref.at[0, table_ref[row, 1]], sem.at[0])
    start_store(table_ref, row, first_ref, second_ref, panel_ref, store)
    end_store(table_ref, row, store)


def in_hbm(array):
    return pltpu.with_memory_space_constraint(array, pltpu.HBM)


def shifted(block, axis, distance):
    devices = range(lax.axis_size(axis))
    route = [(i - distance, i) for i in devices if i - distance in devices]
    return lax.ppermute(block, axis, route)


def ring(block, distance):
    count = lax.axis_size("layer")
    return lax.ppermute(block, "layer", [(i, (i + distance) % count) for i in range(count)])


def per_device(top_trace, sources, near_blocks, near_index, far_left, far_right, assign):
    panel_count, _, rows, columns = top_trace.shape
    rank = far_left.shape[2]
    near = near_index.shape[1]
    blocks_dev = rows // BLK
    width = columns // PARTS
    lanes = 2 * width
    reach_rows = BAND * BLK
    reach_shards = -(-reach_rows // rows)
    layer_count = lax.axis_size("layer")
    layer_pos = lax.axis_index("layer")
    iface_count = lax.axis_size("iface")
    iface_pos = lax.axis_index("iface")
    chunk_count = panel_count * PARTS
    tick_count = chunk_count + 2 * (layer_count - 1)
    in_pairs = iface_count == 4 and reach_rows <= rows
    is_odd = iface_pos % 2

    offset = near_index - iface_pos * blocks_dev
    own = jnp.logical_and(offset >= 0, offset < blocks_dev)
    if in_pairs:
        below = jnp.where(is_odd == 1, blocks_dev, blocks_dev + BAND)
        above = jnp.where(is_odd == 1, blocks_dev + BAND, blocks_dev)
        slot = jnp.where(own, offset, jnp.where(offset < 0, below + offset + BAND, above + offset - blocks_dev))
    else:
        shard = jnp.floor_divide(offset, blocks_dev)
        group = jnp.where(shard < 0, -shard, jnp.where(shard > 0, reach_shards + shard, 0))
        slot = group * blocks_dev + offset - shard * blocks_dev
    key = jnp.where(own, 0, near) + jnp.arange(near)[None, :]
    place = jnp.sum(key[:, None, :] < key[:, :, None], axis=2)
    hit = place[:, None, :] == jnp.arange(near)[None, :, None]
    slot = jnp.sum(jnp.where(hit, slot[:, None, :], 0), axis=2).astype(jnp.int32)
    order = jnp.sum(jnp.where(hit, jnp.arange(near)[None, None, :], 0), axis=2).astype(jnp.int32)
    own_offsets = [min(b, BAND) + min(blocks_dev - 1 - b, BAND) + 1 for b in range(blocks_dev)]
    early = tuple(max(0, min(near, count - (2 * BAND + 1 - near))) for count in own_offsets)
    early_flops, late_flops = sum(early), near * blocks_dev - sum(early)

    next_right = ring(far_right, -1)[0].reshape(2 * rank, rows)
    bank = in_hbm(sources[0])
    smem = pl.BlockSpec(memory_space=pltpu.SMEM)
    vmem = pl.BlockSpec(memory_space=pltpu.VMEM)
    anywhere = pl.BlockSpec(memory_space=pl.ANY)
    params = pltpu.CompilerParams(vmem_limit_bytes=VMEM_LIMIT)
    buffer_rows = rows + rank
    own_right = in_hbm(far_right[0].reshape(2 * rank, rows))

    def enter(panels):
        chunks = PARTS * len(panels)
        return pl.pallas_call(
            functools.partial(enter_kernel, rank, panels),
            out_shape=[pltpu.VMEM((buffer_rows, lanes), jnp.bfloat16)] * chunks,
            in_specs=[anywhere, anywhere],
            out_specs=[vmem] * chunks,
            scratch_shapes=[
                pltpu.VMEM((len(panels), 2, rows, columns), jnp.bfloat16),
                pltpu.VMEM((2 * rank, rows), jnp.bfloat16),
                pltpu.SemaphoreType.DMA((len(panels) + 1,)),
            ],
            compiler_params=params,
            name="enter",
        )(in_hbm(top_trace), own_right)

    top = list(enter((0,)))
    left_mat = pl.pallas_call(
        transpose_kernel,
        out_shape=pltpu.VMEM((rows, 2 * rank), jnp.bfloat16),
        in_specs=[vmem],
        out_specs=vmem,
        compiler_params=params,
        name="turn_left",
    )(far_left[0].reshape(2 * rank, rows))
    blocks_mat = in_hbm(near_blocks[0])
    pair_flops = 2 * 2 * BLK * BLK * 256

    table_shape = (tick_count + 1, 2 * near)
    panel = jnp.floor_divide(lax.broadcasted_iota(jnp.int32, table_shape, 0) - 2 * layer_pos, PARTS)
    column = lax.broadcasted_iota(jnp.int32, table_shape, 1)
    held_panel = jnp.clip(panel, 0, panel_count - 1)
    own_layer = lax.broadcasted_iota(jnp.int32, assign.shape, 0) == layer_pos
    own_assign = jnp.sum(jnp.where(own_layer, assign, 0), axis=0)
    each_panel = lax.broadcasted_iota(jnp.int32, (1, 1, panel_count), 2)
    bank_pos = jnp.sum(jnp.where(held_panel[:, :, None] == each_panel, own_assign[None, None, :], 0), axis=2)
    valid = jnp.logical_and(panel >= 1, panel <= panel_count).astype(jnp.int32)
    stored_panel = jnp.clip(panel - 1, 0, panel_count - 1)
    scalars = jnp.where(column == 0, bank_pos, jnp.where(column == 1, stored_panel, valid))
    table = jnp.concatenate([jnp.concatenate([slot, order], axis=1), scalars]).astype(jnp.int32)
    table, is_first = lax.optimization_barrier((table, layer_pos == 0))

    def exchange(entering):
        if in_pairs:
            split = reach_rows // 2
            near_half = lax.dynamic_slice_in_dim(entering, (1 - is_odd) * (rows - reach_rows), reach_rows)
            far_start = is_odd * (rows - reach_rows)
            far_first = lax.dynamic_slice_in_dim(entering, far_start, split)
            far_last = lax.dynamic_slice_in_dim(entering, far_start + split, split)
            parts = entering[rows:]
            swap = [(i, i ^ 1) for i in range(iface_count)]
            inner = lax.ppermute(jnp.concatenate([far_first, parts]), "iface", swap)
            near_halo = lax.ppermute(near_half, "iface", swap)
            pair_sum = parts.astype(jnp.float32) + inner[split:].astype(jnp.float32)
            is_inner = jnp.logical_or(iface_pos == 1, iface_pos == 2)
            crossing = jnp.concatenate(
                [
                    jnp.where(is_inner, far_last, inner[:split]),
                    pair_sum.astype(jnp.bfloat16),
                ]
            )
            outer = lax.ppermute(crossing, "iface", [(i, iface_count - 1 - i) for i in range(iface_count)])
            pieces = ((0, 0, reach_rows), (3, 0, split), (2, 0, split))
            return [near_halo, inner, outer], pieces, ((1, split), (2, split))
        trace = entering[:rows]
        parts = entering[rows:].astype(jnp.float32)
        others = lax.psum(parts, "iface") - parts
        distances = [d for d in range(1, reach_shards + 1)]
        halos = [shifted(trace, "iface", d) for d in distances] + [shifted(trace, "iface", -d) for d in distances]
        pieces = tuple((at, 0, rows) for at in range(len(halos)))
        return halos + [others], pieces, ((len(halos), 0),)

    leaving = []
    arrived = None
    stored = None
    for tick in range(tick_count):
        first = top[min(tick, chunk_count - 1)]
        entering = first if tick < 2 else jnp.where(is_first, first, arrived)
        arrived = shifted(updated, "layer", 1) if 0 < tick < tick_count - 1 else None
        more, pieces, parts_at = exchange(entering)
        window_rows = rows + sum(count for _, _, count in pieces)
        window = pltpu.VMEM((window_rows, lanes), jnp.bfloat16)
        with_store = tick >= PARTS and tick % PARTS == 0
        operands = [table, blocks_mat, entering, bank]
        in_specs = [smem, anywhere if tick == 0 else vmem, vmem, anywhere]
        shapes = [pltpu.VMEM((rows, lanes), jnp.float32), window, window]
        out_specs = [vmem] * 3
        scratch = [pltpu.VMEM((2, rows, columns), jnp.bfloat16)]
        aliases = {}
        if with_store:
            operands += [leaving[tick - 2], leaving[tick - 1]]
            in_specs += [vmem, vmem]
            if stored is not None:
                aliases = {len(operands): 3}
                operands.append(stored)
                in_specs.append(anywhere)
            shapes.append(pltpu.HBM((1,) + top_trace.shape, jnp.bfloat16))
            out_specs.append(anywhere)
            scratch.append(pltpu.VMEM((2, rows, columns), jnp.bfloat16))
        scratch.append(pltpu.SemaphoreType.DMA((2,)))
        if tick == 0:
            shapes.append(pltpu.VMEM(near_blocks.shape[1:], jnp.bfloat16))
            out_specs.append(vmem)
            scratch.append(pltpu.SemaphoreType.DMA((2, blocks_dev)))
        result = pl.pallas_call(
            functools.partial(own_kernel, tick, early, near, with_store),
            out_shape=shapes,
            in_specs=in_specs,
            out_specs=out_specs,
            scratch_shapes=scratch,
            input_output_aliases=aliases,
            compiler_params=params,
            cost_estimate=pl.CostEstimate(
                flops=pair_flops * early_flops // COST_CUT, bytes_accessed=rows * columns // COST_CUT, transcendentals=0
            ),
            name="own_blocks",
        )(*operands)
        acc, window_own, turned_own = result[:3]
        if tick == 0:
            blocks_mat = result[3]
        if with_store:
            stored = result[3]
        if in_pairs:
            acc, more[-1] = lax.optimization_barrier((acc, more[-1]))
            swap = [(i, i ^ 1) for i in range(iface_count)]
            more.append(lax.ppermute(more[-1][: reach_rows // 2], "iface", swap))
        updated = pl.pallas_call(
            functools.partial(rest_kernel, early, near, pieces, parts_at, rank),
            out_shape=[pltpu.VMEM((buffer_rows, lanes), jnp.bfloat16), window, window],
            in_specs=[smem] + [vmem] * (7 + len(more)),
            out_specs=[vmem] * 3,
            input_output_aliases={6 + len(more): 1, 7 + len(more): 2},
            compiler_params=params,
            cost_estimate=pl.CostEstimate(
                flops=pair_flops * late_flops // COST_CUT, bytes_accessed=rows * lanes // COST_CUT, transcendentals=0
            ),
            name="other_blocks",
        )(table, blocks_mat, acc, entering, left_mat, next_right, *more, window_own, turned_own)[0]
        if tick == 0 and panel_count > 1:
            top += enter(tuple(range(1, panel_count)))
        following = min(tick + 1, chunk_count - 1)
        if arrived is not None:
            kept, arrived, top[following] = lax.optimization_barrier((updated, arrived, top[following]))
        else:
            kept, top[following] = lax.optimization_barrier((updated, top[following]))
        leaving.append(kept)

    return pl.pallas_call(
        functools.partial(store_kernel, blocks_dev + tick_count),
        out_shape=jax.ShapeDtypeStruct((1,) + top_trace.shape, jnp.bfloat16),
        in_specs=[smem, vmem, vmem, anywhere],
        out_specs=anywhere,
        scratch_shapes=[pltpu.VMEM((2, rows, columns), jnp.bfloat16), pltpu.SemaphoreType.DMA((1,))],
        input_output_aliases={3: 0},
        compiler_params=params,
        name="last_panel",
    )(table, leaving[-2], leaving[-1], stored)


def solution(mesh):
    return jax.shard_map(
        per_device,
        mesh=mesh,
        in_specs=(
            P("groups", None, "iface", None),
            P("layer", "groups", None, "iface", None),
            P("layer", None, "iface", None, None, None),
            P("iface", None),
            P("layer", None, None, "iface"),
            P("layer", None, None, "iface"),
            P(),
        ),
        out_specs=P("layer", "groups", None, "iface", None),
        check_vma=False,
    )
```
